128 devices in a mesh: rows: 16 (over x, z_hi, core), blk: 8 (over z_lo, y).
Axes of the slice: x: 4, y: 4, z: 4 (z_hi: 2, z_lo: 2; z = z_hi * 2 + z_lo), core: 2. Of those that a mesh axis runs over, the one named last changes fastest.
Arguments:
- p2_tiles: bfloat16 [16, 8, 128, 16384], P('rows', 'blk'), may hold values from -6 to 6
- window_tiles: bfloat16 [8, 64, 16384], P('blk'), may hold values from -0.09375 to 0.09375
- square_tiles: bfloat16 [16, 8, 64, 16384], P('rows', 'blk'), may hold values from -4 to 4
- pairs: int32 [16, 8, 8, 2, 256], P('rows', 'blk'), may hold values from -1 to 127, as said below
- tasks: int32 [16, 8, 16, 16, 3], P('rows', 'blk'), may hold values from -1 to 63, as said below
- basis: bfloat16 [16, 32, 128, 128], P('rows'), may hold values from -0.052978516 to 0.052978516
Outputs:
- purified: bfloat16 [16, 8, 64, 16384], P('rows', 'blk')
- density_grid: float32 [2048], P(('rows', 'blk'))
The draws below stay inside these ranges and needn't reach their ends.
Inputs may be any that keep to these rules, and one draw needn't show every extreme that they name: Row 0 holds -1 or an A tile below 128; row 1 a window tile below 64. The share of live pairs differs between devices. `tasks`: tile ids are -1 or below 64, live slots come first; basis ids are below 32. Some owner receives 16 live slots from every device.
All inputs are finite; a program needn't handle non-finite values.
Results may differ from the reference program's by a relative error of at most 0.0029.
Values may be sent and summed in bfloat16 or wider, within the bound.
No kernel may reach another device: no remote copies, remote signals or barrier semaphores. Data moves between devices by JAX's collectives and lax.ppermute only.
A program may use at most 320 MiB of HBM per device.

```python
import jax
import jax.numpy as jnp
from jax import lax

BS = 128
A_TILES = 128
B_TILES = 64
C_TILES = 64
KSTEP = 4
SLOT = 16
NBAS = 32
G_SLAB = 128
N_ROWS = 16
N_BLK = 8


def draw_pairs(key, part):
    key = jax.random.fold_in(key, 11)
    keys = jax.random.split(key, 4)
    shape = (N_ROWS, N_BLK, N_BLK, C_TILES * KSTEP)
    share = jax.random.randint(keys[0], (N_ROWS, N_BLK, 1, 1), 30, 101)
    live = jax.random.randint(keys[1], shape, 0, 100) < share
    left = jnp.where(live, jax.random.randint(keys[2], shape, 0, A_TILES), -1)
    right = jax.random.randint(keys[3], shape, 0, B_TILES)
    left = left.at[0, 0, 0, 0].set(A_TILES - 1)
    left = left.at[0, 0, 0, 1].set(-1)
    right = right.at[0, 0, 0, 0].set(B_TILES - 1)
    return jnp.stack([left, right], axis=3).astype(jnp.int32)


def draw_tasks(key, part):
    key = jax.random.fold_in(key, 23)
    keys = jax.random.split(key, 5)
    counts = jax.random.randint(keys[0], (N_ROWS, N_BLK, N_ROWS), 1, SLOT + 1)
    busy = jax.random.randint(keys[1], (), 0, N_ROWS)
    owners = jnp.arange(N_ROWS, dtype=jnp.int32)
    counts = jnp.where(owners == busy, SLOT, counts)
    counts = counts.at[0, 0, (busy + 1) % N_ROWS].set(1)
    shape = (N_ROWS, N_BLK, N_ROWS, SLOT)
    slots = jnp.arange(SLOT, dtype=jnp.int32)
    tile_ids = jax.random.randint(keys[2], shape, 0, C_TILES)
    tile_ids = jnp.where(slots < counts[..., None], tile_ids, -1)
    tile_ids = tile_ids.at[0, 0, busy, 0].set(C_TILES - 1)
    row_ids = jax.random.randint(keys[3], shape, 0, NBAS)
    col_ids = jax.random.randint(keys[4], shape, 0, NBAS)
    row_ids = row_ids.at[0, 0, 0, 0].set(NBAS - 1)
    return jnp.stack([tile_ids, row_ids, col_ids], axis=4).astype(jnp.int32)


def level_of(stream_key, shape, cuts, low, largest):
    factor_of, own = 1.0, jax.random.fold_in(stream_key, 6)
    for position, parts in cuts:
        steps = jnp.exp(jax.random.uniform(jax.random.fold_in(own, position), (parts,), jnp.float32, low / len(cuts), largest / len(cuts)))
        factor_of = factor_of * jnp.repeat(steps, shape[position] // parts).reshape([-1 if axis == position else 1 for axis in range(len(shape))])
    return factor_of


def bell_draw(key, shape, deviation, most, cuts=(), kind=jnp.bfloat16):
    gain = level_of(key, shape, cuts, -0.22, 0.18) if cuts else 1.0
    values = jax.random.normal(key, shape, jnp.float32) * deviation * gain
    return jnp.minimum(jnp.maximum(values, -most), most).astype(kind)


def setup_inputs(seed: int = 0) -> dict:
    streams_of = jax.random.split(jax.random.key(seed), 7)
    return {
        "p2_tiles": bell_draw(streams_of[0], (N_ROWS, N_BLK, A_TILES, BS * BS), 1.0, 6.0, ((0, 16), (1, 8))),
        "window_tiles": bell_draw(streams_of[1], (N_BLK, B_TILES, BS * BS), (BS * KSTEP * N_BLK) ** -0.5, 0.09375, ((0, 8),)),
        "square_tiles": bell_draw(streams_of[2], (N_ROWS, N_BLK, C_TILES, BS * BS), 0.3, 4.0, ((0, 16), (1, 8))),
        "pairs": draw_pairs(jax.random.fold_in(streams_of[6], 71), 0),
        "tasks": draw_tasks(jax.random.fold_in(streams_of[6], 71), 0),
        "basis": bell_draw(streams_of[5], (N_ROWS, NBAS, BS, G_SLAB), 0.0088, 0.052978516, ((0, 16),)),
    }


def reference(p2_tiles, window_tiles, square_tiles, pairs, tasks, basis):
    devices = N_ROWS * N_BLK
    left_all = p2_tiles.reshape(devices, A_TILES, BS * BS)
    square_all = square_tiles.reshape(devices, C_TILES, BS * BS)
    pair_all = pairs.reshape(devices, N_BLK, 2, C_TILES * KSTEP)

    def one_device(index):
        column = index % N_BLK
        a_tiles = left_all[index]
        plan = pair_all[index]
        total = jnp.zeros((C_TILES, BS, BS), jnp.float32)
        for offset in range(N_BLK):
            source = (column - offset) % N_BLK
            piece = window_tiles[source]
            left = plan[offset, 0]
            right = plan[offset, 1]
            gathered_a = jnp.take(a_tiles, jnp.maximum(left, 0), axis=0)
            gathered_a = jnp.where((left >= 0)[:, None], gathered_a, jnp.zeros_like(gathered_a))
            gathered_b = jnp.take(piece, right, axis=0)
            lhs = gathered_a.reshape(C_TILES, KSTEP, BS, BS).astype(jnp.float32)
            rhs = gathered_b.reshape(C_TILES, KSTEP, BS, BS).astype(jnp.float32)
            total = total + jnp.einsum('ckij,ckjl->cil', lhs, rhs)
        square = square_all[index].reshape(C_TILES, BS, BS).astype(jnp.float32)
        return (3.0 * square - 2.0 * total).astype(jnp.bfloat16)

    purified_all = lax.map(one_device, jnp.arange(devices, dtype=jnp.int32))
    flat_tiles = purified_all.reshape(devices, C_TILES, BS * BS)
    task_all = tasks.reshape(devices, N_ROWS, SLOT, 3)
    owners = jnp.arange(N_ROWS, dtype=jnp.int32)[:, None]

    def add_device(carry, item):
        tiles, task = item
        tile_ids = task[..., 0]
        outgoing = jnp.take(tiles, jnp.maximum(tile_ids, 0), axis=0)
        outgoing = jnp.where((tile_ids >= 0)[..., None], outgoing, jnp.zeros_like(outgoing))
        mats = outgoing.reshape(N_ROWS, SLOT, BS, BS).astype(jnp.float32)
        row_basis = basis[owners, task[..., 1]].astype(jnp.float32)
        col_basis = basis[owners, task[..., 2]].astype(jnp.float32)
        spread = jnp.einsum('stij,stjg->stig', mats, col_basis)
        values = jnp.sum(row_basis * spread, axis=2)
        return carry + jnp.sum(values, axis=1), None

    start = jnp.zeros((N_ROWS, G_SLAB), jnp.float32)
    grid, unused = lax.scan(add_device, start, (flat_tiles, task_all))
    purified = purified_all.reshape(N_ROWS, N_BLK, C_TILES, BS * BS)
    return purified, grid.reshape(N_ROWS * G_SLAB)
```

```python
import jax
import jax.numpy as jnp
from jax import lax
from jax.experimental import pallas as pl
from jax.experimental.pallas import tpu as pltpu
from jax.sharding import Mesh
from jax.sharding import PartitionSpec as P

BS = 128
A_TILES = 128
B_TILES = 64
C_TILES = 64
KSTEP = 4
SLOT = 16
NBAS = 32
OWNERS = 16
HALF = 32
ROWS = ("x", "zh", "core")
BLK = ("zl", "y")
MIB = 1 << 20


def around(value, axis):
    pairs = []
    for core in range(2):
        for place in range(4):
            to = (place + 1) % 4 if core == 0 else (place + 3) % 4
            if axis == "x":
                pairs.append((place * 2 + core, to * 2 + core))
            else:
                pairs.append((core * 4 + place, core * 4 + to))
    return lax.ppermute(value, ("x", "core") if axis == "x" else ("core", axis), pairs)


def across(value, axes):
    count = 2 ** len(axes)
    return lax.ppermute(value, axes, [(i, count - 1 - i) for i in range(count)])


def swapped(value):
    return across(value, ("core",))


def gather_shares(mine, other, axis, link):
    near_a = around(mine, axis)
    pair_a = across(mine, link)
    near_b = around(other, axis)
    pair_b = swapped(pair_a)
    far_a = around(near_a, axis)
    pnear_a = around(pair_a, axis)
    pfar_a = across(far_a, link)
    pnear_b = around(pair_b, axis)
    return [
        mine, other, near_a, near_b, swapped(near_a), swapped(near_b), far_a, swapped(far_a),
        pair_a, pair_b, pnear_a, pnear_b, swapped(pnear_a), swapped(pnear_b), pfar_a, swapped(pfar_a),
    ]


def slot_of(pair, hop, half, core):
    rel = half ^ core
    ahead = jnp.where(core == 0, 3, 1)
    place = jnp.where(hop == 0, rel, jnp.where(hop == 2, 6 + rel, jnp.where(hop == ahead, 2 + rel, 5 - rel)))
    return pair * 8 + place


def tile_sums(total, c, group, first, a_ref, w_ref, left_ref, right_ref):
    for share in range(first, first + group):
        for k in range(0, KSTEP, 2):
            at = share * (C_TILES * KSTEP) + c * KSTEP + k
            lhs = jnp.concatenate([a_ref[left_ref[at]], a_ref[left_ref[at + 1]]], axis=1)
            rhs = jnp.concatenate([w_ref[right_ref[at]], w_ref[right_ref[at + 1]]], axis=0)
            total = total + jnp.dot(lhs, rhs, preferred_element_type=jnp.float32)
    return total


def early_kernel(count, left_ref, right_ref, a_hbm, *rest):
    pieces = rest[: 2 * count]
    out_ref, a_ref, w_ref, sems = rest[2 * count :]
    copies = [pltpu.make_async_copy(a_hbm, a_ref.at[pl.ds(0, A_TILES)], sems.at[0])]
    for i, piece in enumerate(pieces):
        copies.append(pltpu.make_async_copy(piece, w_ref.at[pl.ds(i * HALF, HALF)], sems.at[1 + i]))
    for copy in copies:
        copy.start()
    a_ref[A_TILES] = jnp.zeros((BS, BS), jnp.bfloat16)
    for copy in copies:
        copy.wait()

    def one(c, carry):
        total = tile_sums(jnp.zeros((BS, BS), jnp.float32), c, count, 0, a_ref, w_ref, left_ref, right_ref)
        out_ref[c] = total
        return carry

    lax.fori_loop(0, C_TILES, one, 0)


def late_kernel(count, left_ref, right_ref, tile_ref, row_ref, col_ref, a_hbm, acc_hbm, sq_hbm, *rest):
    pieces = rest[: 2 * count]
    slabs = rest[2 * count : 2 * count + 16]
    out_ref, grid_ref, a_ref, w_ref, acc_ref, sq_ref, p_ref, b_ref, sems = rest[2 * count + 16 :]
    copies = [
        pltpu.make_async_copy(a_hbm, a_ref.at[pl.ds(0, A_TILES)], sems.at[0]),
        pltpu.make_async_copy(acc_hbm, acc_ref, sems.at[1]),
        pltpu.make_async_copy(sq_hbm, sq_ref, sems.at[2]),
    ]
    for i, piece in enumerate(pieces):
        copies.append(pltpu.make_async_copy(piece, w_ref.at[pl.ds(i * HALF, HALF)], sems.at[3 + i]))
    tables = []
    for i, slab in enumerate(slabs):
        tables.append(pltpu.make_async_copy(slab, b_ref.at[pl.ds(i * NBAS, NBAS)], sems.at[3 + 2 * count + i]))
    for copy in copies + tables:
        copy.start()
    a_ref[A_TILES] = jnp.zeros((BS, BS), jnp.bfloat16)
    p_ref[C_TILES] = jnp.zeros((BS, BS), jnp.bfloat16)
    for copy in copies:
        copy.wait()

    def one(c, carry):
        total = tile_sums(acc_ref[c], c, count, 0, a_ref, w_ref, left_ref, right_ref)
        pure = (3.0 * sq_ref[c].astype(jnp.float32) - 2.0 * total).astype(jnp.bfloat16)
        p_ref[c] = pure
        out_ref[c] = pure
        return carry

    lax.fori_loop(0, C_TILES, one, 0)
    for copy in tables:
        copy.wait()

    def owner(s, carry):
        live = jnp.int32(0)
        for t in range(SLOT):
            live = live + jnp.where(tile_ref[s * SLOT + t] < C_TILES, 1, 0)

        def four(g, total):
            for t in range(4):
                at = s * SLOT + g * 4 + t
                spread = jnp.dot(p_ref[tile_ref[at]], b_ref[col_ref[at]], preferred_element_type=jnp.float32)
                total = total + b_ref[row_ref[at]].astype(jnp.float32) * spread
            return total

        total = lax.fori_loop(0, (live + 3) // 4, four, jnp.zeros((BS, BS), jnp.float32))
        grid_ref[pl.ds(s, 1), :] = jnp.sum(total, axis=0, keepdims=True)
        return carry

    lax.fori_loop(0, OWNERS, owner, 0)


def smem():
    return pl.BlockSpec(memory_space=pltpu.SMEM)


def hbm():
    return pl.BlockSpec(memory_space=pl.ANY)


def vmem():
    return pl.BlockSpec(memory_space=pltpu.VMEM)


def early_product(left, right, a_tiles, pieces):
    count = len(pieces) // 2
    flops = 2 * count * C_TILES * KSTEP * BS**3
    return pl.pallas_call(
        lambda *refs: early_kernel(count, *refs),
        out_shape=jax.ShapeDtypeStruct((C_TILES, BS, BS), jnp.float32),
        in_specs=[smem(), smem(), hbm()] + [hbm()] * len(pieces),
        out_specs=vmem(),
        scratch_shapes=[
            pltpu.VMEM((A_TILES + 1, BS, BS), jnp.bfloat16),
            pltpu.VMEM((len(pieces) * HALF, BS, BS), jnp.bfloat16),
            pltpu.SemaphoreType.DMA((1 + len(pieces),)),
        ],
        compiler_params=pltpu.CompilerParams(vmem_limit_bytes=24 * MIB),
        cost_estimate=pl.CostEstimate(flops=3 * flops, bytes_accessed=(8 + len(pieces)) * MIB, transcendentals=0),
        name="early_product",
    )(left, right, a_tiles, *pieces)


def late_product(left, right, tile, row, col, a_tiles, acc, square, pieces, slabs):
    count = len(pieces) // 2
    flops = 2 * count * C_TILES * KSTEP * BS**3
    return pl.pallas_call(
        lambda *refs: late_kernel(count, *refs),
        out_shape=(
            jax.ShapeDtypeStruct((C_TILES, BS, BS), jnp.bfloat16),
            jax.ShapeDtypeStruct((OWNERS, BS), jnp.float32),
        ),
        in_specs=[smem()] * 5 + [hbm()] * 3 + [hbm()] * (len(pieces) + len(slabs)),
        out_specs=(vmem(), vmem()),
        scratch_shapes=[
            pltpu.VMEM((A_TILES + 1, BS, BS), jnp.bfloat16),
            pltpu.VMEM((len(pieces) * HALF, BS, BS), jnp.bfloat16),
            pltpu.VMEM((C_TILES, BS, BS), jnp.float32),
            pltpu.VMEM((C_TILES, BS, BS), jnp.bfloat16),
            pltpu.VMEM((C_TILES + 1, BS, BS), jnp.bfloat16),
            pltpu.VMEM((OWNERS * NBAS, BS, BS), jnp.bfloat16),
            pltpu.SemaphoreType.DMA((3 + len(pieces) + len(slabs),)),
        ],
        compiler_params=pltpu.CompilerParams(vmem_limit_bytes=48 * MIB),
        cost_estimate=pl.CostEstimate(flops=3 * flops, bytes_accessed=40 * MIB, transcendentals=0),
        name="late_product",
    )(left, right, tile, row, col, a_tiles, acc, square, *pieces, *slabs)


EARLY_SLOTS = (0, 1, 2, 3, 4, 5, 6, 7, 8, 9)
LATE_SLOTS = (10, 11, 12, 13, 14, 15)
EARLY_SHARES = ((0, 0), (0, 1), (0, 3), (0, 2), (1, 0))
LATE_SHARES = ((1, 1), (1, 3), (1, 2))


def plans(pairs, core, zl, y, shares, slots):
    lefts, rights = [], []
    for pair, hop in shares:
        source = (zl ^ pair) * 4 + ((y + hop) & 3)
        step = ((zl * 4 + y) - source) & 7
        plan = lax.dynamic_index_in_dim(pairs, step, 0, keepdims=False)
        tile = plan[1]
        slot = slot_of(pair, jnp.int32(hop), tile // HALF, core) - slots[0]
        lefts.append(jnp.where(plan[0] < 0, A_TILES, plan[0]))
        rights.append(slot * HALF + tile % HALF)
    return jnp.concatenate(lefts), jnp.concatenate(rights)


def body(p2_tiles, window_tiles, square_tiles, pairs, tasks, basis):
    core = lax.axis_index("core")
    x, zh, zl, y = (lax.axis_index(name) for name in ("x", "zh", "zl", "y"))
    slab = basis[0]
    share = window_tiles[0]
    mine = lax.dynamic_slice_in_dim(share, core * HALF, HALF, 0).reshape(HALF, BS, BS)
    other = lax.dynamic_slice_in_dim(share, (1 - core) * HALF, HALF, 0).reshape(HALF, BS, BS)
    window = gather_shares(mine, other, "y", ("zl",))
    tables = gather_shares(slab, swapped(slab), "x", ("zh", "zl"))

    a_tiles = p2_tiles[0, 0].reshape(A_TILES, BS, BS)
    square = square_tiles[0, 0].reshape(C_TILES, BS, BS)
    early = plans(pairs[0, 0], core, zl, y, EARLY_SHARES, EARLY_SLOTS)
    late = plans(pairs[0, 0], core, zl, y, LATE_SHARES, LATE_SLOTS)

    task = tasks[0, 0]
    owner = jnp.arange(OWNERS, dtype=jnp.int32)[:, None]
    place = slot_of((owner // 2 % 2) ^ zh, (owner // 4 - x) & 3, owner % 2, core) * NBAS
    tile = jnp.where(task[..., 0] < 0, C_TILES, task[..., 0]).reshape(-1)
    row = (place + jnp.clip(task[..., 1], 0, NBAS - 1)).reshape(-1)
    col = (place + jnp.clip(task[..., 2], 0, NBAS - 1)).reshape(-1)

    acc = early_product(*early, a_tiles, [window[i] for i in EARLY_SLOTS])
    pure, grid = late_product(*late, tile, row, col, a_tiles, acc, square, [window[i] for i in LATE_SLOTS], tables)
    parts = lax.all_to_all(grid.reshape(128, 16), ROWS + BLK, split_axis=0, concat_axis=0, tiled=True)
    return pure.reshape(1, 1, C_TILES, BS * BS), jnp.sum(parts, axis=0)


def solution(mesh):
    split = Mesh(mesh.devices.reshape(4, 2, 2, 2, 4), ("x", "zh", "core", "zl", "y"))
    return jax.shard_map(
        body,
        mesh=split,
        in_specs=(
            P(ROWS, BLK, None, None),
            P(BLK, None, None),
            P(ROWS, BLK, None, None),
            P(ROWS, BLK, None, None, None),
            P(ROWS, BLK, None, None, None),
            P(ROWS, None, None, None),
        ),
        out_specs=(P(ROWS, BLK, None, None), P(ROWS + BLK)),
        check_vma=False,
    )
```

```python
import jax
import jax.numpy as jnp
from jax import lax
from jax.experimental import pallas as pl
from jax.experimental.pallas import tpu as pltpu
from jax.sharding import Mesh
from jax.sharding import PartitionSpec as P

BS = 128
A_TILES = 128
B_TILES = 64
C_TILES = 64
KSTEP = 4
SLOT = 16
NBAS = 32
OWNERS = 16
HALF = 32
UNROLL = 16
TASKS = 8
ROWS = ("x", "zh", "core")
BLK = ("zl", "y")
MIB = 1 << 20
VMEM = 60 * MIB


def around(value, axis):
    pairs = []
    for core in range(2):
        for place in range(4):
            to = (place + 1) % 4 if core == 0 else (place + 3) % 4
            if axis == "x":
                pairs.append((place * 2 + core, to * 2 + core))
            else:
                pairs.append((core * 4 + place, core * 4 + to))
    return lax.ppermute(value, ("x", "core") if axis == "x" else ("core", axis), pairs)


def across(value, axes):
    count = 2 ** len(axes)
    return lax.ppermute(value, axes, [(i, count - 1 - i) for i in range(count)])


def swapped(value):
    return across(value, ("core",))


def half_of(share, core):
    return lax.dynamic_slice_in_dim(share, core * HALF, HALF, 0)


def gate(values, deps=()):
    count = len(values)
    return pl.pallas_call(
        lambda *refs: None,
        out_shape=tuple(jax.ShapeDtypeStruct(value.shape, value.dtype) for value in values),
        in_specs=[hbm()] * (count + len(deps)),
        out_specs=(hbm(),) * count,
        input_output_aliases={i: i for i in range(count)},
        compiler_params=pltpu.CompilerParams(vmem_limit_bytes=VMEM),
        name="gate",
    )(*values, *deps)


def slot_of(pair, hop, half, core):
    rel = half ^ core
    place = jnp.where(hop == ahead_of(core), 2 + rel, 5 - rel)
    return pair * 8 + jnp.where(hop == 0, rel, jnp.where(hop == 2, 6 + rel, place))


def ahead_of(core):
    return jnp.where(core == 0, 3, 1)


def tile_sum(c, share, a_ref, w_ref, left_ref, right_ref):
    total = None
    for k in range(0, KSTEP, 2):
        at = share * (C_TILES * KSTEP) + c * KSTEP + k
        lhs = jnp.concatenate([a_ref[left_ref[at]], a_ref[left_ref[at + 1]]], axis=1)
        rhs = jnp.concatenate([w_ref[right_ref[at]], w_ref[right_ref[at + 1]]], axis=0)
        term = jnp.dot(lhs, rhs, preferred_element_type=jnp.float32)
        total = term if total is None else total + term
    return total


def sums(sizes, count, first, refs, outs, last, square=None):
    left_ref, right_ref, a_hbm, pieces, acc_hbm, a_ref, w_ref, sum_ref, sems, others = refs
    tiles = pltpu.make_async_copy(a_hbm, a_ref.at[pl.ds(0, A_TILES)], sems.at[0])
    needs, at = [[] for _ in range(count)], 0
    for i, (size, piece) in enumerate(zip(sizes, pieces)):
        needs[at // B_TILES].append(pltpu.make_async_copy(piece, w_ref.at[pl.ds(at, size)], sems.at[2 + i]))
        at += size
    needs[0].append(tiles)
    if not first:
        needs[0].append(pltpu.make_async_copy(acc_hbm, sum_ref, sems.at[1]))
    for need in needs:
        for copy in need:
            copy.start()
    for copy in others:
        copy.start()
    a_ref[A_TILES] = jnp.zeros((BS, BS), jnp.bfloat16)
    if square is not None:
        needs[-1].append(square)
    for share in range(count):
        for copy in needs[share]:
            copy.wait()

        def some(g, carry, share=share):
            for u in range(UNROLL):
                c = g * UNROLL + u
                total = tile_sum(c, share, a_ref, w_ref, left_ref, right_ref)
                if share > 0 or not first:
                    total = total + sum_ref[c]
                if share < count - 1:
                    sum_ref[c] = total
                else:
                    outs(c, total)
            if share == count - 1:
                last(g)
            return carry

        lax.fori_loop(0, C_TILES // UNROLL, some, 0)


def product_kernel(sizes, count, first, left_ref, right_ref, a_hbm, *rest):
    pieces = rest[: len(sizes)]
    rest = list(rest[len(sizes) :])
    acc_hbm = None if first else rest.pop(0)
    out_hbm, out_ref, a_ref, w_ref, sum_ref, sems, out_sems = rest

    def put(part):
        span = pl.ds(part * UNROLL, UNROLL)
        return pltpu.make_async_copy(out_ref.at[span], out_hbm.at[span], out_sems.at[part])

    def outs(c, total):
        out_ref[c] = total

    refs = (left_ref, right_ref, a_hbm, pieces, acc_hbm, a_ref, w_ref, sum_ref, sems, [])
    sums(sizes, count, first, refs, outs, lambda g: put(g).start())
    for part in range(C_TILES // UNROLL):
        put(part).wait()


def final_kernel(sizes, count, slab_sizes, left_ref, right_ref, who_ref, tile_ref, row_ref, col_ref, a_hbm, *rest):
    pieces, rest = rest[: len(sizes)], rest[len(sizes) :]
    acc_hbm, sq_hbm = rest[:2]
    slabs, rest = rest[2 : 2 + len(slab_sizes)], rest[2 + len(slab_sizes) :]
    out_hbm, grid_ref, a_ref, w_ref, sum_ref, sq_ref, p_ref, b_ref, sems, out_sems, slab_sems = rest

    def bring(source, slot):
        return pltpu.make_async_copy(source, b_ref.at[pl.ds(slot * NBAS, NBAS)], slab_sems.at[slot])

    square = pltpu.make_async_copy(sq_hbm, sq_ref, out_sems.at[C_TILES // UNROLL])
    others, slot = [square], 0
    for size, slab in zip(slab_sizes, slabs):
        for part in range(size // NBAS):
            others.append(bring(slab.at[pl.ds(part * NBAS, NBAS)], slot))
            slot += 1

    def put(part):
        span = pl.ds(part * UNROLL, UNROLL)
        return pltpu.make_async_copy(p_ref.at[span], out_hbm.at[span], out_sems.at[part])

    def outs(c, total):
        p_ref[c] = (3.0 * sq_ref[c].astype(jnp.float32) - 2.0 * total).astype(jnp.bfloat16)

    p_ref[C_TILES] = jnp.zeros((BS, BS), jnp.bfloat16)
    refs = (left_ref, right_ref, a_hbm, pieces, acc_hbm, a_ref, w_ref, sum_ref, sems, others)
    sums(sizes, count, False, refs, outs, lambda g: put(g).start(), square)

    def one(slot, carry):
        s = who_ref[slot]
        live = jnp.int32(0)
        for t in range(SLOT):
            live = live + jnp.where(tile_ref[s * SLOT + t] < C_TILES, 1, 0)
        bring(slabs[0].at[pl.ds(0, NBAS)], slot).wait()

        def some(g, total):
            for t in range(TASKS):
                at = s * SLOT + g * TASKS + t
                spread = jnp.dot(p_ref[tile_ref[at]], b_ref[col_ref[at]], preferred_element_type=jnp.float32)
                total = total + b_ref[row_ref[at]].astype(jnp.float32) * spread
            return total

        total = lax.fori_loop(0, (live + TASKS - 1) // TASKS, some, jnp.zeros((BS, BS), jnp.float32))
        grid_ref[pl.ds(s, 1), :] = jnp.sum(total, axis=0, keepdims=True)
        return carry

    lax.fori_loop(0, OWNERS, one, 0)
    for part in range(C_TILES // UNROLL):
        put(part).wait()


def smem():
    return pl.BlockSpec(memory_space=pltpu.SMEM)


def hbm():
    return pl.BlockSpec(memory_space=pl.ANY)


def vmem():
    return pl.BlockSpec(memory_space=pltpu.VMEM)


def product(plan, a_tiles, pieces, acc=None):
    sizes = [piece.shape[0] for piece in pieces]
    count = sum(sizes) // B_TILES
    operands = [*plan, a_tiles, *pieces] + ([] if acc is None else [acc])
    return pl.pallas_call(
        lambda *refs: product_kernel(sizes, count, acc is None, *refs),
        out_shape=jax.ShapeDtypeStruct((C_TILES, BS, BS), jnp.float32),
        in_specs=[smem(), smem()] + [hbm()] * (len(operands) - 2),
        out_specs=hbm(),
        scratch_shapes=[
            pltpu.VMEM((C_TILES, BS, BS), jnp.float32),
            pltpu.VMEM((A_TILES + 1, BS, BS), jnp.bfloat16),
            pltpu.VMEM((sum(sizes), BS, BS), jnp.bfloat16),
            pltpu.VMEM((C_TILES, BS, BS), jnp.float32),
            pltpu.SemaphoreType.DMA((2 + len(pieces),)),
            pltpu.SemaphoreType.DMA((C_TILES // UNROLL,)),
        ],
        compiler_params=pltpu.CompilerParams(vmem_limit_bytes=VMEM),
        cost_estimate=pl.CostEstimate(
            flops=4 * count * C_TILES * KSTEP * BS**3, bytes_accessed=(12 + 2 * count) * MIB, transcendentals=0
        ),
        name="product",
    )(*operands)


def final(plan, who, tile, row, col, a_tiles, pieces, acc, square, slabs):
    sizes = [piece.shape[0] for piece in pieces]
    count = sum(sizes) // B_TILES
    slab_sizes = [slab.shape[0] for slab in slabs]
    return pl.pallas_call(
        lambda *refs: final_kernel(sizes, count, slab_sizes, *refs),
        out_shape=(
            jax.ShapeDtypeStruct((C_TILES, BS, BS), jnp.bfloat16),
            jax.ShapeDtypeStruct((OWNERS, BS), jnp.float32),
        ),
        in_specs=[smem()] * 6 + [hbm()] * (3 + len(pieces) + len(slabs)),
        out_specs=(hbm(), vmem()),
        scratch_shapes=[
            pltpu.VMEM((A_TILES + 1, BS, BS), jnp.bfloat16),
            pltpu.VMEM((sum(sizes), BS, BS), jnp.bfloat16),
            pltpu.VMEM((C_TILES, BS, BS), jnp.float32),
            pltpu.VMEM((C_TILES, BS, BS), jnp.bfloat16),
            pltpu.VMEM((C_TILES + 1, BS, BS), jnp.bfloat16),
            pltpu.VMEM((OWNERS * NBAS, BS, BS), jnp.bfloat16),
            pltpu.SemaphoreType.DMA((2 + len(pieces),)),
            pltpu.SemaphoreType.DMA((C_TILES // UNROLL + 1,)),
            pltpu.SemaphoreType.DMA((OWNERS,)),
        ],
        compiler_params=pltpu.CompilerParams(vmem_limit_bytes=VMEM),
        cost_estimate=pl.CostEstimate(
            flops=4 * (count * C_TILES * KSTEP + 512) * BS**3, bytes_accessed=40 * MIB, transcendentals=0
        ),
        name="final",
    )(*plan, who, tile, row, col, a_tiles, *pieces, acc, square, *slabs)


def plans(pairs, core, zl, y, shares):
    lefts, rights = [], []
    for at, (pair, hop, turned) in enumerate(shares):
        source = (zl ^ pair) * 4 + ((y + hop) & 3)
        step = ((zl * 4 + y) - source) & 7
        plan = lax.dynamic_index_in_dim(pairs, step, 0, keepdims=False)
        half = (plan[1] // HALF) ^ core ^ turned
        lefts.append(jnp.where(plan[0] < 0, A_TILES, plan[0]))
        rights.append(at * B_TILES + half * HALF + plan[1] % HALF)
    return jnp.concatenate(lefts), jnp.concatenate(rights)


def body(p2_tiles, window_tiles, square_tiles, pairs, tasks, basis):
    core = lax.axis_index("core")
    x, zh, zl, y = (lax.axis_index(name) for name in ("x", "zh", "zl", "y"))
    slab = basis[0]
    share = window_tiles[0]
    mine = half_of(share, core).reshape(HALF, BS, BS)
    other = half_of(share, 1 - core).reshape(HALF, BS, BS)
    a_tiles = p2_tiles[0, 0].reshape(A_TILES, BS, BS)
    square = square_tiles[0, 0].reshape(C_TILES, BS, BS)
    ahead = ahead_of(core)
    stages = (
        ((0, 0, 0), (0, ahead, 0), (0, 4 - ahead, 1), (0, 2, 0), (1, 0, 0)),
        ((1, ahead, 0),),
        ((1, 4 - ahead, 1), (1, 2, 0)),
    )
    plan = [plans(pairs[0, 0], core, zl, y, stage) for stage in stages]
    task = tasks[0, 0]
    owner = jnp.arange(OWNERS, dtype=jnp.int32)[:, None]
    place = slot_of((owner // 2 % 2) ^ zh, (owner // 4 - x) & 3, owner % 2, core) * NBAS
    tile = jnp.where(task[..., 0] < 0, C_TILES, task[..., 0]).reshape(-1)
    row = (place + jnp.clip(task[..., 1], 0, NBAS - 1)).reshape(-1)
    col = (place + jnp.clip(task[..., 2], 0, NBAS - 1)).reshape(-1)

    slots = jnp.arange(16, dtype=jnp.int32)[:, None]
    who = jnp.sum(jnp.where(place // NBAS == slots.T, owner, 0), axis=0)
    link, zz = ("zl",), ("zh", "zl")
    near_a, bnear_a = around(mine, "y"), around(slab, "x")
    pair, bpair = across(mine, link), across(slab, zz)
    bother = swapped(slab)
    near_b, bnear_b = around(other, "y"), around(bother, "x")
    work = [tile, row, col, who, *[index for both in plan for index in both], a_tiles]
    near_a, near_b, pair, bpair, bnear_a, bnear_b = gate([near_a, near_b, pair, bpair, bnear_a, bnear_b], work)
    far, bfar = around(near_a, "y"), around(bnear_a, "x")
    spair, sbpair = swapped(pair), swapped(bpair)
    snear_a, snear_b = swapped(near_a), swapped(near_b)
    both, bboth = jnp.concatenate([pair, spair]), jnp.concatenate([bpair, sbpair])
    both, bboth, far, bfar, bnear_a, bnear_b = gate(
        [both, bboth, far, bfar, bnear_a, bnear_b], [snear_a, snear_b, square]
    )
    pnear, bpnear = around(both, "y"), around(bboth, "x")
    pfar, bpfar = across(far, link), across(bfar, zz)
    sfar = swapped(far)
    acc = product(plan[0], a_tiles, [mine, other, near_a, near_b, snear_a, snear_b, far, sfar, both])
    sbnear_a, sbnear_b, sbfar = swapped(bnear_a), swapped(bnear_b), swapped(bfar)
    pnear, bpnear, pfar, bpfar = gate([pnear, bpnear, pfar, bpfar], [acc, sbnear_a, sbnear_b, sbfar])
    spnear, spfar, sbpfar, sbpnear = swapped(pnear), swapped(pfar), swapped(bpfar), swapped(bpnear)
    acc = product(plan[1], a_tiles, [pnear], acc)
    tables = [
        slab, bother, bnear_a, bnear_b, sbnear_a, sbnear_b, bfar, sbfar, bboth, bpnear, sbpnear, bpfar, sbpfar,
    ]
    pure, grid = final(plan[2], who, tile, row, col, a_tiles, [spnear, pfar, spfar], acc, square, tables)
    parts = lax.all_to_all(grid.reshape(128, 16), ROWS + BLK, split_axis=0, concat_axis=0, tiled=True)
    return pure.reshape(1, 1, C_TILES, BS * BS), jnp.sum(parts, axis=0)


def solution(mesh):
    split = Mesh(mesh.devices.reshape(4, 2, 2, 2, 4), ("x", "zh", "core", "zl", "y"))
    return jax.shard_map(
        body,
        mesh=split,
        in_specs=(
            P(ROWS, BLK, None, None),
            P(BLK, None, None),
            P(ROWS, BLK, None, None),
            P(ROWS, BLK, None, None, None),
            P(ROWS, BLK, None, None, None),
            P(ROWS, None, None, None),
        ),
        out_specs=(P(ROWS, BLK, None, None), P(ROWS + BLK)),
        check_vma=False,
    )
```

```python
import jax
import jax.numpy as jnp
from jax import lax
from jax.experimental import pallas as pl
from jax.experimental.pallas import tpu as pltpu
from jax.sharding import Mesh
from jax.sharding import PartitionSpec as P

BS = 128
A_TILES = 128
B_TILES = 64
C_TILES = 64
KSTEP = 4
SLOT = 16
NBAS = 32
OWNERS = 16
HALF = 32
UNROLL = 16
ROWS = ("x", "zh", "core")
BLK = ("zl", "y")
MIB = 1 << 20


def around(value, axis):
    pairs = []
    for core in range(2):
        for place in range(4):
            to = (place + 1) % 4 if core == 0 else (place + 3) % 4
            if axis == "x":
                pairs.append((place * 2 + core, to * 2 + core))
            else:
                pairs.append((core * 4 + place, core * 4 + to))
    return lax.ppermute(value, ("x", "core") if axis == "x" else ("core", axis), pairs)


def across(value, axes):
    count = 2 ** len(axes)
    return lax.ppermute(value, axes, [(i, count - 1 - i) for i in range(count)])


def swapped(value):
    return across(value, ("core",))


def half_of(share, core):
    return lax.dynamic_slice_in_dim(share, core * HALF, HALF, 0)


def matrices(flat):
    return flat.reshape(flat.shape[0], BS, BS)


def gate(values, deps=()):
    count = len(values)
    return pl.pallas_call(
        lambda *refs: None,
        out_shape=tuple(jax.ShapeDtypeStruct(value.shape, value.dtype) for value in values),
        in_specs=[hbm()] * (count + len(deps)),
        out_specs=(hbm(),) * count,
        input_output_aliases={i: i for i in range(count)},
        compiler_params=pltpu.CompilerParams(vmem_limit_bytes=MIB),
        name="gate",
    )(*values, *deps)


def slot_of(pair, hop, half, core):
    rel = half ^ core
    place = jnp.where(hop == ahead_of(core), 2 + rel, 5 - rel)
    return pair * 8 + jnp.where(hop == 0, rel, jnp.where(hop == 2, 6 + rel, place))


def ahead_of(core):
    return jnp.where(core == 0, 3, 1)


def tile_sum(c, share, a_ref, w_ref, left_ref, right_ref):
    total = None
    for k in range(0, KSTEP, 2):
        at = share * (C_TILES * KSTEP) + c * KSTEP + k
        lhs = jnp.concatenate([a_ref[left_ref[at]], a_ref[left_ref[at + 1]]], axis=1)
        rhs = jnp.concatenate([w_ref[right_ref[at]], w_ref[right_ref[at + 1]]], axis=0)
        term = jnp.dot(lhs, rhs, preferred_element_type=jnp.float32)
        total = term if total is None else total + term
    return total


def sums(sizes, count, refs, start, outs):
    left_ref, right_ref, a_ref, pieces, w_ref, sum_ref, sems = refs
    needs, at = [[] for _ in range(count)], 0
    for i, (size, piece) in enumerate(zip(sizes, pieces)):
        needs[at // B_TILES].append(pltpu.make_async_copy(piece, w_ref.at[pl.ds(at, size)], sems.at[i]))
        at += size
    for need in needs:
        for copy in need:
            copy.start()
    w_ref[count * B_TILES] = jnp.zeros((BS, BS), jnp.bfloat16)
    for share in range(count):
        for copy in needs[share]:
            copy.wait()

        def some(g, carry, share=share):
            for u in range(UNROLL):
                c = g * UNROLL + u
                total = tile_sum(c, share, a_ref, w_ref, left_ref, right_ref)
                before = sum_ref[c] if share > 0 else start(c)
                if before is not None:
                    total = total + before
                if share < count - 1:
                    sum_ref[c] = total
                else:
                    outs(g, u, total)
            return carry

        lax.fori_loop(0, C_TILES // UNROLL, some, 0)


def product_kernel(sizes, count, first, left_ref, right_ref, a_ref, *rest):
    pieces = rest[: len(sizes)]
    rest = list(rest[len(sizes) :])
    acc_ref = None if first else rest.pop(0)
    out_ref, w_ref, sems = rest

    def outs(g, u, total):
        out_ref[g * UNROLL + u] = total

    refs = (left_ref, right_ref, a_ref, pieces, w_ref, out_ref, sems)
    sums(sizes, count, refs, lambda c: None if first else acc_ref[c], outs)


def final_kernel(sizes, count, slab_sizes, left_ref, right_ref, who_ref, tile_ref, row_ref, col_ref, a_ref, *rest):
    pieces, rest = rest[: len(sizes)], rest[len(sizes) :]
    acc_ref, sq_ref = rest[:2]
    slabs, rest = rest[2 : 2 + len(slab_sizes)], rest[2 + len(slab_sizes) :]
    out_hbm, grid_ref, w_ref, sum_ref, p_ref, sems, out_sems = rest

    def put(part):
        span = pl.ds(part * UNROLL, UNROLL)
        return pltpu.make_async_copy(p_ref.at[span], out_hbm.at[span], out_sems.at[part])

    def outs(g, u, total):
        c = g * UNROLL + u
        p_ref[c] = (3.0 * sq_ref[c].astype(jnp.float32) - 2.0 * total).astype(jnp.bfloat16)
        if u == UNROLL - 1:
            put(g).start()

    p_ref[C_TILES] = jnp.zeros((BS, BS), jnp.bfloat16)
    refs = (left_ref, right_ref, a_ref, pieces, w_ref, sum_ref, sems)
    sums(sizes, count, refs, lambda c: acc_ref[c], outs)

    slot = 0
    for size, slab in zip(slab_sizes, slabs):
        base = slot * NBAS
        for _ in range(size // NBAS):
            s = who_ref[slot]
            total = None
            for t in range(SLOT):
                at = s * SLOT + t
                spread = jnp.dot(p_ref[tile_ref[at]], slab[col_ref[at] - base], preferred_element_type=jnp.float32)
                term = slab[row_ref[at] - base].astype(jnp.float32) * spread
                total = term if total is None else total + term
            grid_ref[pl.ds(s, 1), :] = jnp.sum(total, axis=0, keepdims=True)
            slot += 1
    for part in range(C_TILES // UNROLL):
        put(part).wait()


def smem():
    return pl.BlockSpec(memory_space=pltpu.SMEM)


def hbm():
    return pl.BlockSpec(memory_space=pl.ANY)


def vmem():
    return pl.BlockSpec(memory_space=pltpu.VMEM)


def product(plan, a_tiles, pieces, acc=None):
    sizes = [piece.shape[0] for piece in pieces]
    count = sum(sizes) // B_TILES
    operands = [*plan, a_tiles, *pieces] + ([] if acc is None else [acc])
    specs = [smem(), smem(), vmem()] + [hbm()] * len(pieces) + ([] if acc is None else [vmem()])
    return pl.pallas_call(
        lambda *refs: product_kernel(sizes, count, acc is None, *refs),
        out_shape=jax.ShapeDtypeStruct((C_TILES, BS, BS), jnp.float32),
        in_specs=specs,
        out_specs=vmem(),
        scratch_shapes=[
            pltpu.VMEM((sum(sizes) + 1, BS, BS), jnp.bfloat16),
            pltpu.SemaphoreType.DMA((len(pieces),)),
        ],
        compiler_params=pltpu.CompilerParams(vmem_limit_bytes=(2 * count + 3) * MIB),
        cost_estimate=pl.CostEstimate(
            flops=4 * count * C_TILES * KSTEP * BS**3, bytes_accessed=(12 + 2 * count) * MIB, transcendentals=0
        ),
        name="product",
    )(*operands)


def final(plan, who, tile, row, col, a_tiles, pieces, acc, square, slabs):
    sizes = [piece.shape[0] for piece in pieces]
    count = sum(sizes) // B_TILES
    slab_sizes = [slab.shape[0] for slab in slabs]
    return pl.pallas_call(
        lambda *refs: final_kernel(sizes, count, slab_sizes, *refs),
        out_shape=(
            jax.ShapeDtypeStruct((C_TILES, BS, BS), jnp.bfloat16),
            jax.ShapeDtypeStruct((OWNERS, BS), jnp.float32),
        ),
        in_specs=[smem()] * 6 + [vmem()] + [hbm()] * len(pieces) + [vmem()] * (2 + len(slabs)),
        out_specs=(pl.BlockSpec(memory_space=pltpu.HBM), vmem()),
        scratch_shapes=[
            pltpu.VMEM((sum(sizes) + 1, BS, BS), jnp.bfloat16),
            pltpu.VMEM((C_TILES, BS, BS), jnp.float32),
            pltpu.VMEM((C_TILES + 1, BS, BS), jnp.bfloat16),
            pltpu.SemaphoreType.DMA((len(pieces),)),
            pltpu.SemaphoreType.DMA((C_TILES // UNROLL,)),
        ],
        compiler_params=pltpu.CompilerParams(vmem_limit_bytes=18 * MIB),
        cost_estimate=pl.CostEstimate(
            flops=4 * (count * C_TILES * KSTEP + 512) * BS**3, bytes_accessed=40 * MIB, transcendentals=0
        ),
        name="final",
    )(*plan, who, tile, row, col, a_tiles, *pieces, acc, square, *slabs)


def plans(pairs, core, zl, y, shares):
    lefts, rights = [], []
    for at, (pair, hop, turned) in enumerate(shares):
        source = (zl ^ pair) * 4 + ((y + hop) & 3)
        step = ((zl * 4 + y) - source) & 7
        plan = lax.dynamic_index_in_dim(pairs, step, 0, keepdims=False)
        half = (plan[1] // HALF) ^ core ^ turned
        lefts.append(jnp.maximum(plan[0], 0))
        rights.append(jnp.where(plan[0] < 0, len(shares) * B_TILES, at * B_TILES + half * HALF + plan[1] % HALF))
    return jnp.concatenate(lefts), jnp.concatenate(rights)


def body(p2_tiles, window_tiles, square_tiles, pairs, tasks, basis):
    core = lax.axis_index("core")
    x, zh, zl, y = (lax.axis_index(name) for name in ("x", "zh", "zl", "y"))
    slab = basis[0]
    share = window_tiles[0]
    raw_mine, raw_other, slab = gate([half_of(share, core), half_of(share, 1 - core), slab])
    mine, other = matrices(raw_mine), matrices(raw_other)
    a_tiles = p2_tiles[0, 0].reshape(A_TILES, BS, BS)
    square = square_tiles[0, 0].reshape(C_TILES, BS, BS)
    ahead = ahead_of(core)
    stages = (
        ((0, 0, 0), (0, ahead, 0), (0, 4 - ahead, 1), (0, 2, 0), (1, 0, 0)),
        ((1, ahead, 0),),
        ((1, 4 - ahead, 1), (1, 2, 0)),
    )
    plan = [plans(pairs[0, 0], core, zl, y, stage) for stage in stages]
    task = tasks[0, 0]
    owner = jnp.arange(OWNERS, dtype=jnp.int32)[:, None]
    place = slot_of((owner // 2 % 2) ^ zh, (owner // 4 - x) & 3, owner % 2, core) * NBAS
    tile = jnp.where(task[..., 0] < 0, C_TILES, task[..., 0]).reshape(-1)
    row = (place + jnp.clip(task[..., 1], 0, NBAS - 1)).reshape(-1)
    col = (place + jnp.clip(task[..., 2], 0, NBAS - 1)).reshape(-1)

    slots = jnp.arange(16, dtype=jnp.int32)[:, None]
    who = jnp.sum(jnp.where(place // NBAS == slots.T, owner, 0), axis=0)
    link, zz = ("zl",), ("zh", "zl")
    raw_near, bnear_a = around(raw_mine, "y"), around(slab, "x")
    pair, bpair = across(mine, link), across(slab, zz)
    bother = swapped(slab)
    near_b, bnear_b = around(other, "y"), around(bother, "x")
    near_a = matrices(raw_near)
    sbnear_a = swapped(bnear_a)
    work = [tile, row, col, who, *[index for both in plan for index in both], a_tiles, sbnear_a]
    raw_near, near_a, near_b, pair, bpair, bnear_a, bnear_b = gate(
        [raw_near, near_a, near_b, pair, bpair, bnear_a, bnear_b], work
    )
    far, bfar = around(raw_near, "y"), around(bnear_a, "x")
    spair, sbpair = swapped(pair), swapped(bpair)
    snear_a, snear_b = swapped(near_a), swapped(near_b)
    both, bboth = jnp.concatenate([pair, spair]), jnp.concatenate([bpair, sbpair])
    both, bboth, far, bfar, bnear_b = gate([both, bboth, far, bfar, bnear_b], [snear_a, snear_b, square])
    far = matrices(far)
    pnear, bpnear = around(both, "y"), around(bboth, "x")
    pfar, bpfar = across(far, link), across(bfar, zz)
    sfar = swapped(far)
    acc = product(plan[0], a_tiles, [mine, other, near_a, near_b, snear_a, snear_b, far, sfar, both])
    (bnear_b,) = gate([bnear_b], [acc])
    sbnear_b, sbfar = swapped(bnear_b), swapped(bfar)
    pnear, bpnear, pfar, bpfar = gate([pnear, bpnear, pfar, bpfar], [acc, sbnear_b, sbfar])
    spnear, spfar, sbpfar, sbpnear = swapped(pnear), swapped(pfar), swapped(bpfar), swapped(bpnear)
    acc = product(plan[1], a_tiles, [pnear], acc)
    tables = [
        slab, bother, bnear_a, bnear_b, sbnear_a, sbnear_b, bfar, sbfar, bboth, bpnear, sbpnear, bpfar, sbpfar,
    ]
    pure, grid = final(plan[2], who, tile, row, col, a_tiles, [spnear, pfar, spfar], acc, square, tables)
    parts = lax.all_to_all(grid.reshape(128, 16), ROWS + BLK, split_axis=0, concat_axis=0, tiled=True)
    return pure.reshape(1, 1, C_TILES, BS * BS), jnp.sum(parts, axis=0)


def solution(mesh):
    split = Mesh(mesh.devices.reshape(4, 2, 2, 2, 4), ("x", "zh", "core", "zl", "y"))
    return jax.shard_map(
        body,
        mesh=split,
        in_specs=(
            P(ROWS, BLK, None, None),
            P(BLK, None, None),
            P(ROWS, BLK, None, None),
            P(ROWS, BLK, None, None, None),
            P(ROWS, BLK, None, None, None),
            P(ROWS, None, None, None),
        ),
        out_specs=(P(ROWS, BLK, None, None), P(ROWS + BLK)),
        check_vma=False,
    )
```

```python
import jax
import jax.numpy as jnp
from jax import lax
from jax.experimental import pallas as pl
from jax.experimental.pallas import tpu as pltpu
from jax.sharding import Mesh
from jax.sharding import PartitionSpec as P

BS = 128
A_TILES = 128
B_TILES = 64
C_TILES = 64
KSTEP = 4
SLOT = 16
NBAS = 32
OWNERS = 16
HALF = 32
UNROLL = 16
ROWS = ("x", "zh", "core")
BLK = ("zl", "y")
MIB = 1 << 20


def around(value, axis):
    pairs = []
    for core in range(2):
        for place in range(4):
            to = (place + 1) % 4 if core == 0 else (place + 3) % 4
            if axis == "x":
                pairs.append((place * 2 + core, to * 2 + core))
            else:
                pairs.append((core * 4 + place, core * 4 + to))
    return lax.ppermute(value, ("x", "core") if axis == "x" else ("core", axis), pairs)


def across(value, axes):
    count = 2 ** len(axes)
    return lax.ppermute(value, axes, [(i, count - 1 - i) for i in range(count)])


def swapped(value):
    return across(value, ("core",))


def half_of(share, core):
    return lax.dynamic_slice_in_dim(share, core * HALF, HALF, 0)


def matrices(flat):
    return flat.reshape(flat.shape[0], BS, BS)


def gate(values, deps=()):
    count = len(values)
    return pl.pallas_call(
        lambda *refs: None,
        out_shape=tuple(jax.ShapeDtypeStruct(value.shape, value.dtype) for value in values),
        in_specs=[hbm()] * (count + len(deps)),
        out_specs=(hbm(),) * count,
        input_output_aliases={i: i for i in range(count)},
        compiler_params=pltpu.CompilerParams(vmem_limit_bytes=MIB),
        name="gate",
    )(*values, *deps)


def slot_of(pair, hop, half, core):
    rel = half ^ core
    place = jnp.where(hop == ahead_of(core), 2 + rel, 5 - rel)
    return pair * 8 + jnp.where(hop == 0, rel, jnp.where(hop == 2, 6 + rel, place))


def ahead_of(core):
    return jnp.where(core == 0, 3, 1)


def tile_sum(c, share, a_ref, w_ref, left_ref, right_ref):
    total = None
    for k in range(0, KSTEP, 2):
        at = share * (C_TILES * KSTEP) + c * KSTEP + k
        lhs = jnp.concatenate([a_ref[left_ref[at]], a_ref[left_ref[at + 1]]], axis=1)
        rhs = jnp.concatenate([w_ref[right_ref[at]], w_ref[right_ref[at + 1]]], axis=0)
        term = jnp.dot(lhs, rhs, preferred_element_type=jnp.float32)
        total = term if total is None else total + term
    return total


def sums(sizes, count, refs, start, outs):
    left_ref, right_ref, a_ref, pieces, w_ref, sum_ref, sems = refs
    needs, at = [[] for _ in range(count)], 0
    for i, (size, piece) in enumerate(zip(sizes, pieces)):
        needs[at // B_TILES].append(pltpu.make_async_copy(piece, w_ref.at[pl.ds(at, size)], sems.at[i]))
        at += size
    for need in needs:
        for copy in need:
            copy.start()
    w_ref[count * B_TILES] = jnp.zeros((BS, BS), jnp.bfloat16)
    for share in range(count):
        for copy in needs[share]:
            copy.wait()

        def some(g, carry, share=share):
            for u in range(UNROLL):
                c = g * UNROLL + u
                total = tile_sum(c, share, a_ref, w_ref, left_ref, right_ref)
                before = sum_ref[c] if share > 0 else start(c)
                if before is not None:
                    total = total + before
                if share < count - 1:
                    sum_ref[c] = total
                else:
                    outs(g, u, total)
            return carry

        lax.fori_loop(0, C_TILES // UNROLL, some, 0)


def product_kernel(sizes, count, first, left_ref, right_ref, a_ref, *rest):
    pieces = rest[: len(sizes)]
    rest = list(rest[len(sizes) :])
    acc_ref = None if first else rest.pop(0)
    out_ref, w_ref, sems = rest

    def outs(g, u, total):
        out_ref[g * UNROLL + u] = total

    refs = (left_ref, right_ref, a_ref, pieces, w_ref, out_ref, sems)
    sums(sizes, count, refs, lambda c: None if first else acc_ref[c], outs)


def final_kernel(sizes, count, slab_sizes, left_ref, right_ref, who_ref, tile_ref, row_ref, col_ref, a_ref, *rest):
    pieces, rest = rest[: len(sizes)], rest[len(sizes) :]
    acc_ref, sq_ref = rest[:2]
    slabs, rest = rest[2 : 2 + len(slab_sizes)], rest[2 + len(slab_sizes) :]
    out_hbm, grid_ref, w_ref, sum_ref, p_ref, sems, out_sems = rest

    def put(part):
        span = pl.ds(part * UNROLL, UNROLL)
        return pltpu.make_async_copy(p_ref.at[span], out_hbm.at[span], out_sems.at[part])

    def outs(g, u, total):
        c = g * UNROLL + u
        p_ref[c] = (3.0 * sq_ref[c].astype(jnp.float32) - 2.0 * total).astype(jnp.bfloat16)
        if u == UNROLL - 1:
            put(g).start()

    p_ref[C_TILES] = jnp.zeros((BS, BS), jnp.bfloat16)
    refs = (left_ref, right_ref, a_ref, pieces, w_ref, sum_ref, sems)
    sums(sizes, count, refs, lambda c: acc_ref[c], outs)

    slot = 0
    for size, slab in zip(slab_sizes, slabs):
        base = slot * NBAS
        for _ in range(size // NBAS):
            s = who_ref[slot]
            total = None
            for t in range(SLOT):
                at = s * SLOT + t
                spread = jnp.dot(p_ref[tile_ref[at]], slab[col_ref[at] - base], preferred_element_type=jnp.float32)
                term = slab[row_ref[at] - base].astype(jnp.float32) * spread
                total = term if total is None else total + term
            grid_ref[pl.ds(s, 1), :] = jnp.sum(total, axis=0, keepdims=True)
            slot += 1
    for part in range(C_TILES // UNROLL):
        put(part).wait()


def smem():
    return pl.BlockSpec(memory_space=pltpu.SMEM)


def hbm():
    return pl.BlockSpec(memory_space=pl.ANY)


def vmem():
    return pl.BlockSpec(memory_space=pltpu.VMEM)


def product(plan, a_tiles, pieces, acc=None):
    sizes = [piece.shape[0] for piece in pieces]
    count = sum(sizes) // B_TILES
    operands = [*plan, a_tiles, *pieces] + ([] if acc is None else [acc])
    specs = [smem(), smem(), vmem()] + [hbm()] * len(pieces) + ([] if acc is None else [vmem()])
    return pl.pallas_call(
        lambda *refs: product_kernel(sizes, count, acc is None, *refs),
        out_shape=jax.ShapeDtypeStruct((C_TILES, BS, BS), jnp.float32),
        in_specs=specs,
        out_specs=vmem(),
        scratch_shapes=[
            pltpu.VMEM((sum(sizes) + 1, BS, BS), jnp.bfloat16),
            pltpu.SemaphoreType.DMA((len(pieces),)),
        ],
        compiler_params=pltpu.CompilerParams(vmem_limit_bytes=(2 * count + 3) * MIB),
        cost_estimate=pl.CostEstimate(
            flops=4 * count * C_TILES * KSTEP * BS**3, bytes_accessed=(12 + 2 * count) * MIB, transcendentals=0
        ),
        name="product",
    )(*operands)


def final(plan, who, tile, row, col, a_tiles, pieces, acc, square, slabs):
    sizes = [piece.shape[0] for piece in pieces]
    count = sum(sizes) // B_TILES
    slab_sizes = [slab.shape[0] for slab in slabs]
    return pl.pallas_call(
        lambda *refs: final_kernel(sizes, count, slab_sizes, *refs),
        out_shape=(
            jax.ShapeDtypeStruct((C_TILES, BS, BS), jnp.bfloat16),
            jax.ShapeDtypeStruct((OWNERS, BS), jnp.float32),
        ),
        in_specs=[smem()] * 6 + [vmem()] + [hbm()] * len(pieces) + [vmem()] * (2 + len(slabs)),
        out_specs=(pl.BlockSpec(memory_space=pltpu.HBM), vmem()),
        scratch_shapes=[
            pltpu.VMEM((sum(sizes) + 1, BS, BS), jnp.bfloat16),
            pltpu.VMEM((C_TILES, BS, BS), jnp.float32),
            pltpu.VMEM((C_TILES + 1, BS, BS), jnp.bfloat16),
            pltpu.SemaphoreType.DMA((len(pieces),)),
            pltpu.SemaphoreType.DMA((C_TILES // UNROLL,)),
        ],
        compiler_params=pltpu.CompilerParams(vmem_limit_bytes=18 * MIB),
        cost_estimate=pl.CostEstimate(
            flops=4 * (count * C_TILES * KSTEP + 512) * BS**3, bytes_accessed=40 * MIB, transcendentals=0
        ),
        name="final",
    )(*plan, who, tile, row, col, a_tiles, *pieces, acc, square, *slabs)


def plans(pairs, core, zl, y, shares):
    lefts, rights = [], []
    for at, (pair, hop, turned) in enumerate(shares):
        source = (zl ^ pair) * 4 + ((y + hop) & 3)
        step = ((zl * 4 + y) - source) & 7
        plan = lax.dynamic_index_in_dim(pairs, step, 0, keepdims=False)
        half = (plan[1] // HALF) ^ core ^ turned
        lefts.append(jnp.maximum(plan[0], 0))
        rights.append(jnp.where(plan[0] < 0, len(shares) * B_TILES, at * B_TILES + half * HALF + plan[1] % HALF))
    return jnp.concatenate(lefts), jnp.concatenate(rights)


def body(p2_tiles, window_tiles, square_tiles, pairs, tasks, basis):
    core = lax.axis_index("core")
    x, zh, zl, y = (lax.axis_index(name) for name in ("x", "zh", "zl", "y"))
    slab = basis[0]
    share = window_tiles[0]
    raw_share, share = share, matrices(share)
    a_tiles = p2_tiles[0, 0].reshape(A_TILES, BS, BS)
    square = square_tiles[0, 0].reshape(C_TILES, BS, BS)
    ahead = ahead_of(core)
    stages = (
        ((0, 0, core), (0, ahead, core), (0, 4 - ahead, core), (1, 0, 0)),
        ((1, ahead, 0), (0, 2, 0)),
        ((1, 4 - ahead, 1), (1, 2, 0)),
    )
    plan = [plans(pairs[0, 0], core, zl, y, stage) for stage in stages]
    task = tasks[0, 0]
    owner = jnp.arange(OWNERS, dtype=jnp.int32)[:, None]
    place = slot_of((owner // 2 % 2) ^ zh, (owner // 4 - x) & 3, owner % 2, core) * NBAS
    tile = jnp.where(task[..., 0] < 0, C_TILES, task[..., 0]).reshape(-1)
    row = (place + jnp.clip(task[..., 1], 0, NBAS - 1)).reshape(-1)
    col = (place + jnp.clip(task[..., 2], 0, NBAS - 1)).reshape(-1)

    slots = jnp.arange(16, dtype=jnp.int32)[:, None]
    who = jnp.sum(jnp.where(place // NBAS == slots.T, owner, 0), axis=0)
    link, zz = ("zl",), ("zh", "zl")
    near, bnear_a = around(raw_share, "y"), around(slab, "x")
    pair, bpair = across(half_of(raw_share, core), link), across(slab, zz)
    bother = swapped(slab)
    bnear_b = around(bother, "x")
    sbnear_a = swapped(bnear_a)
    work = [tile, row, col, who, *[index for both in plan for index in both], a_tiles, share, sbnear_a]
    near, pair, bpair, bnear_a, bnear_b = gate([near, pair, bpair, bnear_a, bnear_b], work)
    far, bfar = around(half_of(near, core), "y"), around(bnear_a, "x")
    near, pair = matrices(near), matrices(pair)
    spair, sbpair, snear = swapped(pair), swapped(bpair), swapped(near)
    both, bboth = jnp.concatenate([pair, spair]), jnp.concatenate([bpair, sbpair])
    both, bboth, far, bfar, bnear_b = gate([both, bboth, far, bfar, bnear_b], [snear, square])
    far = matrices(far)
    pnear, bpnear = around(both, "y"), around(bboth, "x")
    pfar, bpfar = across(far, link), across(bfar, zz)
    acc = product(plan[0], a_tiles, [share, near, snear, both])
    bnear_b, far = gate([bnear_b, far], [acc])
    sbnear_b, sbfar, sfar = swapped(bnear_b), swapped(bfar), swapped(far)
    pnear, bpnear, pfar, bpfar = gate([pnear, bpnear, pfar, bpfar], [acc, sfar, sbnear_b, sbfar])
    spnear, spfar, sbpfar, sbpnear = swapped(pnear), swapped(pfar), swapped(bpfar), swapped(bpnear)
    acc = product(plan[1], a_tiles, [pnear, far, sfar], acc)
    tables = [
        slab, bother, bnear_a, bnear_b, sbnear_a, sbnear_b, bfar, sbfar, bboth, bpnear, sbpnear, bpfar, sbpfar,
    ]
    pure, grid = final(plan[2], who, tile, row, col, a_tiles, [spnear, pfar, spfar], acc, square, tables)
    parts = lax.all_to_all(grid.reshape(128, 16), ROWS + BLK, split_axis=0, concat_axis=0, tiled=True)
    return pure.reshape(1, 1, C_TILES, BS * BS), jnp.sum(parts, axis=0)


def solution(mesh):
    split = Mesh(mesh.devices.reshape(4, 2, 2, 2, 4), ("x", "zh", "core", "zl", "y"))
    return jax.shard_map(
        body,
        mesh=split,
        in_specs=(
            P(ROWS, BLK, None, None),
            P(BLK, None, None),
            P(ROWS, BLK, None, None),
            P(ROWS, BLK, None, None, None),
            P(ROWS, BLK, None, None, None),
            P(ROWS, None, None, None),
        ),
        out_specs=(P(ROWS, BLK, None, None), P(ROWS + BLK)),
        check_vma=False,
    )
```

```python
import jax
import jax.numpy as jnp
from jax import lax
from jax.experimental import pallas as pl
from jax.experimental.pallas import tpu as pltpu
from jax.sharding import Mesh
from jax.sharding import PartitionSpec as P

BS = 128
A_TILES = 128
B_TILES = 64
C_TILES = 64
KSTEP = 4
SLOT = 16
NBAS = 32
OWNERS = 16
HALF = 32
UNROLL = 16
ROWS = ("x", "zh", "core")
BLK = ("zl", "y")
MIB = 1 << 20


def around(value, axis):
    pairs = []
    for core in range(2):
        for place in range(4):
            to = (place + 1) % 4 if core == 0 else (place + 3) % 4
            if axis == "x":
                pairs.append((place * 2 + core, to * 2 + core))
            else:
                pairs.append((core * 4 + place, core * 4 + to))
    return lax.ppermute(value, ("x", "core") if axis == "x" else ("core", axis), pairs)


def across(value, axes):
    count = 2 ** len(axes)
    return lax.ppermute(value, axes, [(i, count - 1 - i) for i in range(count)])


def swapped(value):
    return across(value, ("core",))


def half_of(share, core):
    return lax.dynamic_slice_in_dim(share, core * HALF, HALF, 0)


def matrices(flat):
    return flat.reshape(flat.shape[0], BS, BS)


def gate(values, deps=()):
    count = len(values)
    return pl.pallas_call(
        lambda *refs: None,
        out_shape=tuple(jax.ShapeDtypeStruct(value.shape, value.dtype) for value in values),
        in_specs=[hbm()] * (count + len(deps)),
        out_specs=(hbm(),) * count,
        input_output_aliases={i: i for i in range(count)},
        compiler_params=pltpu.CompilerParams(vmem_limit_bytes=MIB),
        name="gate",
    )(*values, *deps)


def slot_of(pair, hop, half, core):
    rel = half ^ core
    place = jnp.where(hop == ahead_of(core), 2 + rel, 5 - rel)
    return pair * 8 + jnp.where(hop == 0, rel, jnp.where(hop == 2, 6 + rel, place))


def ahead_of(core):
    return jnp.where(core == 0, 3, 1)


def tile_sum(c, share, a_ref, w_ref, left_ref, right_ref):
    total = None
    for k in range(0, KSTEP, 2):
        at = share * (C_TILES * KSTEP) + c * KSTEP + k
        lhs = jnp.concatenate([a_ref[left_ref[at]], a_ref[left_ref[at + 1]]], axis=1)
        rhs = jnp.concatenate([w_ref[right_ref[at]], w_ref[right_ref[at + 1]]], axis=0)
        term = jnp.dot(lhs, rhs, preferred_element_type=jnp.float32)
        total = term if total is None else total + term
    return total


def sums(sizes, count, refs, start, outs):
    left_ref, right_ref, a_ref, pieces, w_ref, sum_ref, sems = refs
    needs, at = [[] for _ in range(count)], 0
    for i, (size, piece) in enumerate(zip(sizes, pieces)):
        needs[at // B_TILES].append(pltpu.make_async_copy(piece, w_ref.at[pl.ds(at, size)], sems.at[i]))
        at += size
    for need in needs:
        for copy in need:
            copy.start()
    w_ref[count * B_TILES] = jnp.zeros((BS, BS), jnp.bfloat16)
    for share in range(count):
        for copy in needs[share]:
            copy.wait()

        def some(g, carry, share=share):
            for u in range(UNROLL):
                c = g * UNROLL + u
                total = tile_sum(c, share, a_ref, w_ref, left_ref, right_ref)
                before = sum_ref[c] if share > 0 else start(c)
                if before is not None:
                    total = total + before
                if share < count - 1:
                    sum_ref[c] = total
                else:
                    outs(g, u, total)
            return carry

        lax.fori_loop(0, C_TILES // UNROLL, some, 0)


def product_kernel(sizes, count, first, left_ref, right_ref, a_ref, *rest):
    pieces = rest[: len(sizes)]
    rest = list(rest[len(sizes) :])
    acc_ref = None if first else rest.pop(0)
    out_ref, w_ref, sems = rest

    def outs(g, u, total):
        out_ref[g * UNROLL + u] = total

    refs = (left_ref, right_ref, a_ref, pieces, w_ref, out_ref, sems)
    sums(sizes, count, refs, lambda c: None if first else acc_ref[c], outs)


def final_kernel(sizes, count, slab_sizes, left_ref, right_ref, who_ref, tile_ref, row_ref, col_ref, a_ref, *rest):
    pieces, rest = rest[: len(sizes)], rest[len(sizes) :]
    acc_ref, sq_ref = rest[:2]
    slabs, rest = rest[2 : 2 + len(slab_sizes)], rest[2 + len(slab_sizes) :]
    out_hbm, grid_ref, w_ref, sum_ref, p_ref, sems, out_sems = rest

    def put(part):
        span = pl.ds(part * UNROLL, UNROLL)
        return pltpu.make_async_copy(p_ref.at[span], out_hbm.at[span], out_sems.at[part])

    def outs(g, u, total):
        c = g * UNROLL + u
        p_ref[c] = (3.0 * sq_ref[c].astype(jnp.float32) - 2.0 * total).astype(jnp.bfloat16)
        if u == UNROLL - 1:
            put(g).start()

    p_ref[C_TILES] = jnp.zeros((BS, BS), jnp.bfloat16)
    refs = (left_ref, right_ref, a_ref, pieces, w_ref, sum_ref, sems)
    sums(sizes, count, refs, lambda c: acc_ref[c], outs)

    slot = 0
    for size, slab in zip(slab_sizes, slabs):
        base = slot * NBAS
        for _ in range(size // NBAS):
            s = who_ref[slot]
            total = None
            for t in range(SLOT):
                at = s * SLOT + t
                spread = jnp.dot(p_ref[tile_ref[at]], slab[col_ref[at] - base], preferred_element_type=jnp.float32)
                term = slab[row_ref[at] - base].astype(jnp.float32) * spread
                total = term if total is None else total + term
            grid_ref[pl.ds(s, 1), :] = jnp.sum(total, axis=0, keepdims=True)
            slot += 1
    for part in range(C_TILES // UNROLL):
        put(part).wait()


def smem():
    return pl.BlockSpec(memory_space=pltpu.SMEM)


def hbm():
    return pl.BlockSpec(memory_space=pl.ANY)


def vmem():
    return pl.BlockSpec(memory_space=pltpu.VMEM)


def product(plan, a_tiles, pieces, acc=None):
    sizes = [piece.shape[0] for piece in pieces]
    count = sum(sizes) // B_TILES
    operands = [*plan, a_tiles, *pieces] + ([] if acc is None else [acc])
    specs = [smem(), smem(), vmem()] + [hbm()] * len(pieces) + ([] if acc is None else [vmem()])
    return pl.pallas_call(
        lambda *refs: product_kernel(sizes, count, acc is None, *refs),
        out_shape=jax.ShapeDtypeStruct((C_TILES, BS, BS), jnp.float32),
        in_specs=specs,
        out_specs=vmem(),
        scratch_shapes=[
            pltpu.VMEM((sum(sizes) + 1, BS, BS), jnp.bfloat16),
            pltpu.SemaphoreType.DMA((len(pieces),)),
        ],
        compiler_params=pltpu.CompilerParams(vmem_limit_bytes=(2 * count + 3) * MIB),
        cost_estimate=pl.CostEstimate(
            flops=4 * count * C_TILES * KSTEP * BS**3, bytes_accessed=(12 + 2 * count) * MIB, transcendentals=0
        ),
        name="product",
    )(*operands)


def final(plan, who, tile, row, col, a_tiles, pieces, acc, square, slabs):
    sizes = [piece.shape[0] for piece in pieces]
    count = sum(sizes) // B_TILES
    slab_sizes = [slab.shape[0] for slab in slabs]
    return pl.pallas_call(
        lambda *refs: final_kernel(sizes, count, slab_sizes, *refs),
        out_shape=(
            jax.ShapeDtypeStruct((C_TILES, BS, BS), jnp.bfloat16),
            jax.ShapeDtypeStruct((OWNERS, BS), jnp.float32),
        ),
        in_specs=[smem()] * 6 + [vmem()] + [hbm()] * len(pieces) + [vmem()] * (2 + len(slabs)),
        out_specs=(pl.BlockSpec(memory_space=pltpu.HBM), vmem()),
        scratch_shapes=[
            pltpu.VMEM((sum(sizes) + 1, BS, BS), jnp.bfloat16),
            pltpu.VMEM((C_TILES, BS, BS), jnp.float32),
            pltpu.VMEM((C_TILES + 1, BS, BS), jnp.bfloat16),
            pltpu.SemaphoreType.DMA((len(pieces),)),
            pltpu.SemaphoreType.DMA((C_TILES // UNROLL,)),
        ],
        compiler_params=pltpu.CompilerParams(vmem_limit_bytes=18 * MIB),
        cost_estimate=pl.CostEstimate(
            flops=4 * (count * C_TILES * KSTEP + 512) * BS**3, bytes_accessed=40 * MIB, transcendentals=0
        ),
        name="final",
    )(*plan, who, tile, row, col, a_tiles, *pieces, acc, square, *slabs)


def plans(pairs, core, zl, y, shares):
    lefts, rights = [], []
    for at, (pair, hop, turned) in enumerate(shares):
        source = (zl ^ pair) * 4 + ((y + hop) & 3)
        step = ((zl * 4 + y) - source) & 7
        plan = lax.dynamic_index_in_dim(pairs, step, 0, keepdims=False)
        half = (plan[1] // HALF) ^ core ^ turned
        lefts.append(jnp.maximum(plan[0], 0))
        rights.append(jnp.where(plan[0] < 0, len(shares) * B_TILES, at * B_TILES + half * HALF + plan[1] % HALF))
    return jnp.concatenate(lefts), jnp.concatenate(rights)


def body(p2_tiles, window_tiles, square_tiles, pairs, tasks, basis):
    core = lax.axis_index("core")
    x, zh, zl, y = (lax.axis_index(name) for name in ("x", "zh", "zl", "y"))
    slab = basis[0]
    share = window_tiles[0]
    raw_share, share = share, matrices(share)
    a_tiles = p2_tiles[0, 0].reshape(A_TILES, BS, BS)
    square = square_tiles[0, 0].reshape(C_TILES, BS, BS)
    ahead = ahead_of(core)
    stages = (
        ((0, 0, core), (0, ahead, core), (0, 4 - ahead, core), (1, 0, 0)),
        ((1, ahead, 0), (0, 2, 0)),
        ((1, 4 - ahead, 1), (1, 2, 0)),
    )
    plan = [plans(pairs[0, 0], core, zl, y, stage) for stage in stages]
    task = tasks[0, 0]
    owner = jnp.arange(OWNERS, dtype=jnp.int32)[:, None]
    place = slot_of((owner // 2 % 2) ^ zh, (owner // 4 - x) & 3, owner % 2, core) * NBAS
    tile = jnp.where(task[..., 0] < 0, C_TILES, task[..., 0]).reshape(-1)
    row = (place + jnp.clip(task[..., 1], 0, NBAS - 1)).reshape(-1)
    col = (place + jnp.clip(task[..., 2], 0, NBAS - 1)).reshape(-1)

    slots = jnp.arange(16, dtype=jnp.int32)[:, None]
    who = jnp.sum(jnp.where(place // NBAS == slots.T, owner, 0), axis=0)
    link, zz = ("zl",), ("zh", "zl")
    near, bnear_a = around(raw_share, "y"), around(slab, "x")
    pair, bpair = across(half_of(raw_share, core), link), across(slab, zz)
    bother = swapped(slab)
    bnear_b = around(bother, "x")
    sbnear_a = swapped(bnear_a)
    work = [tile, row, col, who, *[index for both in plan for index in both], a_tiles, share, sbnear_a]
    near, pair, bpair, bnear_a, bnear_b = gate([near, pair, bpair, bnear_a, bnear_b], work)
    far, bfar = around(half_of(near, core), "y"), around(bnear_a, "x")
    spair, sbpair, snear = swapped(pair), swapped(bpair), swapped(near)
    both, bboth = matrices(jnp.concatenate([pair, spair])), jnp.concatenate([bpair, sbpair])
    near, snear = matrices(near), matrices(snear)
    both, bboth, far, bfar, bnear_b = gate([both, bboth, far, bfar, bnear_b], [near, snear, square])
    far = matrices(far)
    pnear, bpnear = around(both, "y"), around(bboth, "x")
    pfar, bpfar = across(far, link), across(bfar, zz)
    acc = product(plan[0], a_tiles, [share, near, snear, both])
    bnear_b, far = gate([bnear_b, far], [acc])
    sbnear_b, sbfar, sfar = swapped(bnear_b), swapped(bfar), swapped(far)
    pnear, bpnear, pfar, bpfar = gate([pnear, bpnear, pfar, bpfar], [acc, sfar, sbnear_b, sbfar])
    spnear, spfar, sbpfar, sbpnear = swapped(pnear), swapped(pfar), swapped(bpfar), swapped(bpnear)
    acc = product(plan[1], a_tiles, [pnear, far, sfar], acc)
    tables = [
        slab, bother, bnear_a, bnear_b, sbnear_a, sbnear_b, bfar, sbfar, bboth, bpnear, sbpnear, bpfar, sbpfar,
    ]
    pure, grid = final(plan[2], who, tile, row, col, a_tiles, [spnear, pfar, spfar], acc, square, tables)
    parts = lax.all_to_all(grid.reshape(128, 16), ROWS + BLK, split_axis=0, concat_axis=0, tiled=True)
    return pure.reshape(1, 1, C_TILES, BS * BS), jnp.sum(parts, axis=0)


def solution(mesh):
    split = Mesh(mesh.devices.reshape(4, 2, 2, 2, 4), ("x", "zh", "core", "zl", "y"))
    return jax.shard_map(
        body,
        mesh=split,
        in_specs=(
            P(ROWS, BLK, None, None),
            P(BLK, None, None),
            P(ROWS, BLK, None, None),
            P(ROWS, BLK, None, None, None),
            P(ROWS, BLK, None, None, None),
            P(ROWS, None, None, None),
        ),
        out_specs=(P(ROWS, BLK, None, None), P(ROWS + BLK)),
        check_vma=False,
    )
```

```python
import jax
import jax.numpy as jnp
from jax import lax
from jax.experimental import pallas as pl
from jax.experimental.pallas import tpu as pltpu
from jax.sharding import Mesh
from jax.sharding import PartitionSpec as P

BS = 128
A_TILES = 128
B_TILES = 64
C_TILES = 64
KSTEP = 4
SLOT = 16
NBAS = 32
OWNERS = 16
HALF = 32
UNROLL = 16
ROWS = ("x", "zh", "core")
BLK = ("zl", "y")
MIB = 1 << 20


def around(value, axis):
    pairs = []
    for core in range(2):
        for place in range(4):
            to = (place + 1) % 4 if core == 0 else (place + 3) % 4
            if axis == "x":
                pairs.append((place * 2 + core, to * 2 + core))
            else:
                pairs.append((core * 4 + place, core * 4 + to))
    return lax.ppermute(value, ("x", "core") if axis == "x" else ("core", axis), pairs)


def across(value, axes):
    count = 2 ** len(axes)
    return lax.ppermute(value, axes, [(i, count - 1 - i) for i in range(count)])


def swapped(value):
    return across(value, ("core",))


def half_of(share, core):
    return lax.dynamic_slice_in_dim(share, core * HALF, HALF, 0)


def half_kernel(core_ref, share_ref, out_ref, sem):
    at = pl.multiple_of(core_ref[0] * HALF, HALF)
    copy = pltpu.make_async_copy(share_ref.at[pl.ds(at, HALF)], out_ref, sem)
    copy.start()
    copy.wait()


def half_copied(share, core):
    return pl.pallas_call(
        half_kernel,
        out_shape=jax.ShapeDtypeStruct((HALF,) + share.shape[1:], share.dtype),
        in_specs=[smem(), hbm()],
        out_specs=hbm(),
        scratch_shapes=[pltpu.SemaphoreType.DMA(())],
        compiler_params=pltpu.CompilerParams(vmem_limit_bytes=MIB),
        name="half",
    )(core.reshape(1), share)


def matrices(flat):
    return flat.reshape(flat.shape[0], BS, BS)


def gate(values, deps=()):
    count = len(values)
    return pl.pallas_call(
        lambda *refs: None,
        out_shape=tuple(jax.ShapeDtypeStruct(value.shape, value.dtype) for value in values),
        in_specs=[hbm()] * (count + len(deps)),
        out_specs=(hbm(),) * count,
        input_output_aliases={i: i for i in range(count)},
        compiler_params=pltpu.CompilerParams(vmem_limit_bytes=MIB),
        name="gate",
    )(*values, *deps)


def slot_of(pair, hop, half, core):
    rel = half ^ core
    place = jnp.where(hop == ahead_of(core), 2 + rel, 5 - rel)
    return pair * 8 + jnp.where(hop == 0, rel, jnp.where(hop == 2, 6 + rel, place))


def ahead_of(core):
    return jnp.where(core == 0, 3, 1)


def tile_sum(c, share, a_ref, w_ref, left_ref, right_ref):
    total = None
    for k in range(0, KSTEP, 2):
        at = share * (C_TILES * KSTEP) + c * KSTEP + k
        lhs = jnp.concatenate([a_ref[left_ref[at]], a_ref[left_ref[at + 1]]], axis=1)
        rhs = jnp.concatenate([w_ref[right_ref[at]], w_ref[right_ref[at + 1]]], axis=0)
        term = jnp.dot(lhs, rhs, preferred_element_type=jnp.float32)
        total = term if total is None else total + term
    return total


def sums(sizes, count, refs, start, outs):
    left_ref, right_ref, a_ref, pieces, w_ref, sum_ref, sems = refs
    needs, at = [[] for _ in range(count)], 0
    for i, (size, piece) in enumerate(zip(sizes, pieces)):
        needs[at // B_TILES].append(pltpu.make_async_copy(piece, w_ref.at[pl.ds(at, size)], sems.at[i]))
        at += size
    for need in needs:
        for copy in need:
            copy.start()
    w_ref[count * B_TILES] = jnp.zeros((BS, BS), jnp.bfloat16)
    for share in range(count):
        for copy in needs[share]:
            copy.wait()

        def some(g, carry, share=share):
            for u in range(UNROLL):
                c = g * UNROLL + u
                total = tile_sum(c, share, a_ref, w_ref, left_ref, right_ref)
                before = sum_ref[c] if share > 0 else start(c)
                if before is not None:
                    total = total + before
                if share < count - 1:
                    sum_ref[c] = total
                else:
                    outs(g, u, total)
            return carry

        lax.fori_loop(0, C_TILES // UNROLL, some, 0)


def product_kernel(sizes, count, first, left_ref, right_ref, a_ref, *rest):
    pieces = rest[: len(sizes)]
    rest = list(rest[len(sizes) :])
    acc_ref = None if first else rest.pop(0)
    out_ref, w_ref, sems = rest

    def outs(g, u, total):
        out_ref[g * UNROLL + u] = total

    refs = (left_ref, right_ref, a_ref, pieces, w_ref, out_ref, sems)
    sums(sizes, count, refs, lambda c: None if first else acc_ref[c], outs)


def final_kernel(sizes, count, slab_sizes, left_ref, right_ref, who_ref, tile_ref, row_ref, col_ref, a_ref, *rest):
    pieces, rest = rest[: len(sizes)], rest[len(sizes) :]
    acc_ref, sq_ref = rest[:2]
    slabs, rest = rest[2 : 2 + len(slab_sizes)], rest[2 + len(slab_sizes) :]
    out_hbm, grid_ref, w_ref, sum_ref, p_ref, sems, out_sems = rest

    def put(part):
        span = pl.ds(part * UNROLL, UNROLL)
        return pltpu.make_async_copy(p_ref.at[span], out_hbm.at[span], out_sems.at[part])

    def outs(g, u, total):
        c = g * UNROLL + u
        p_ref[c] = (3.0 * sq_ref[c].astype(jnp.float32) - 2.0 * total).astype(jnp.bfloat16)
        if u == UNROLL - 1:
            put(g).start()

    p_ref[C_TILES] = jnp.zeros((BS, BS), jnp.bfloat16)
    refs = (left_ref, right_ref, a_ref, pieces, w_ref, sum_ref, sems)
    sums(sizes, count, refs, lambda c: acc_ref[c], outs)

    slot = 0
    for size, slab in zip(slab_sizes, slabs):
        base = slot * NBAS
        for _ in range(size // NBAS):
            s = who_ref[slot]
            total = None
            for t in range(SLOT):
                at = s * SLOT + t
                spread = jnp.dot(p_ref[tile_ref[at]], slab[col_ref[at] - base], preferred_element_type=jnp.float32)
                term = slab[row_ref[at] - base].astype(jnp.float32) * spread
                total = term if total is None else total + term
            grid_ref[pl.ds(s, 1), :] = jnp.sum(total, axis=0, keepdims=True)
            slot += 1
    for part in range(C_TILES // UNROLL):
        put(part).wait()


def smem():
    return pl.BlockSpec(memory_space=pltpu.SMEM)


def hbm():
    return pl.BlockSpec(memory_space=pl.ANY)


def vmem():
    return pl.BlockSpec(memory_space=pltpu.VMEM)


def product(plan, a_tiles, pieces, acc=None):
    sizes = [piece.shape[0] for piece in pieces]
    count = sum(sizes) // B_TILES
    operands = [*plan, a_tiles, *pieces] + ([] if acc is None else [acc])
    specs = [smem(), smem(), vmem()] + [hbm()] * len(pieces) + ([] if acc is None else [vmem()])
    return pl.pallas_call(
        lambda *refs: product_kernel(sizes, count, acc is None, *refs),
        out_shape=jax.ShapeDtypeStruct((C_TILES, BS, BS), jnp.float32),
        in_specs=specs,
        out_specs=vmem(),
        scratch_shapes=[
            pltpu.VMEM((sum(sizes) + 1, BS, BS), jnp.bfloat16),
            pltpu.SemaphoreType.DMA((len(pieces),)),
        ],
        compiler_params=pltpu.CompilerParams(vmem_limit_bytes=(2 * count + 3) * MIB),
        cost_estimate=pl.CostEstimate(
            flops=4 * count * C_TILES * KSTEP * BS**3, bytes_accessed=(12 + 2 * count) * MIB, transcendentals=0
        ),
        name="product",
    )(*operands)


def final(plan, who, tile, row, col, a_tiles, pieces, acc, square, slabs):
    sizes = [piece.shape[0] for piece in pieces]
    count = sum(sizes) // B_TILES
    slab_sizes = [slab.shape[0] for slab in slabs]
    return pl.pallas_call(
        lambda *refs: final_kernel(sizes, count, slab_sizes, *refs),
        out_shape=(
            jax.ShapeDtypeStruct((C_TILES, BS, BS), jnp.bfloat16),
            jax.ShapeDtypeStruct((OWNERS, BS), jnp.float32),
        ),
        in_specs=[smem()] * 6 + [vmem()] + [hbm()] * len(pieces) + [vmem()] * (2 + len(slabs)),
        out_specs=(pl.BlockSpec(memory_space=pltpu.HBM), vmem()),
        scratch_shapes=[
            pltpu.VMEM((sum(sizes) + 1, BS, BS), jnp.bfloat16),
            pltpu.VMEM((C_TILES, BS, BS), jnp.float32),
            pltpu.VMEM((C_TILES + 1, BS, BS), jnp.bfloat16),
            pltpu.SemaphoreType.DMA((len(pieces),)),
            pltpu.SemaphoreType.DMA((C_TILES // UNROLL,)),
        ],
        compiler_params=pltpu.CompilerParams(vmem_limit_bytes=18 * MIB),
        cost_estimate=pl.CostEstimate(
            flops=4 * (count * C_TILES * KSTEP + 512) * BS**3, bytes_accessed=40 * MIB, transcendentals=0
        ),
        name="final",
    )(*plan, who, tile, row, col, a_tiles, *pieces, acc, square, *slabs)


def plans(pairs, core, zl, y, shares):
    lefts, rights = [], []
    for at, (pair, hop, turned) in enumerate(shares):
        source = (zl ^ pair) * 4 + ((y + hop) & 3)
        step = ((zl * 4 + y) - source) & 7
        plan = lax.dynamic_index_in_dim(pairs, step, 0, keepdims=False)
        half = (plan[1] // HALF) ^ core ^ turned
        lefts.append(jnp.maximum(plan[0], 0))
        rights.append(jnp.where(plan[0] < 0, len(shares) * B_TILES, at * B_TILES + half * HALF + plan[1] % HALF))
    return jnp.concatenate(lefts), jnp.concatenate(rights)


def body(p2_tiles, window_tiles, square_tiles, pairs, tasks, basis):
    core = lax.axis_index("core")
    x, zh, zl, y = (lax.axis_index(name) for name in ("x", "zh", "zl", "y"))
    slab = basis[0]
    share = window_tiles[0]
    raw_share, share = share, matrices(share)
    a_tiles = p2_tiles[0, 0].reshape(A_TILES, BS, BS)
    square = square_tiles[0, 0].reshape(C_TILES, BS, BS)
    ahead = ahead_of(core)
    stages = (
        ((0, 0, core), (0, ahead, core), (0, 4 - ahead, core), (1, 0, 0)),
        ((1, ahead, 0), (0, 2, 0)),
        ((1, 4 - ahead, 1), (1, 2, 0)),
    )
    plan = [plans(pairs[0, 0], core, zl, y, stage) for stage in stages]
    task = tasks[0, 0]
    owner = jnp.arange(OWNERS, dtype=jnp.int32)[:, None]
    place = slot_of((owner // 2 % 2) ^ zh, (owner // 4 - x) & 3, owner % 2, core) * NBAS
    tile = jnp.where(task[..., 0] < 0, C_TILES, task[..., 0]).reshape(-1)
    row = (place + jnp.clip(task[..., 1], 0, NBAS - 1)).reshape(-1)
    col = (place + jnp.clip(task[..., 2], 0, NBAS - 1)).reshape(-1)

    slots = jnp.arange(16, dtype=jnp.int32)[:, None]
    who = jnp.sum(jnp.where(place // NBAS == slots.T, owner, 0), axis=0)
    link, zz = ("zl",), ("zh", "zl")
    near, bnear_a = around(raw_share, "y"), around(slab, "x")
    pair, bpair = across(half_copied(raw_share, core), link), across(slab, zz)
    bother = swapped(slab)
    bnear_b = around(bother, "x")
    sbnear_a = swapped(bnear_a)
    work = [tile, row, col, who, *[index for both in plan for index in both], a_tiles, share, sbnear_a]
    near, pair, bpair, bnear_a, bnear_b = gate([near, pair, bpair, bnear_a, bnear_b], work)
    far, bfar = around(half_of(near, core), "y"), around(bnear_a, "x")
    spair, sbpair, snear = swapped(pair), swapped(bpair), swapped(near)
    both, bboth = matrices(jnp.concatenate([pair, spair])), jnp.concatenate([bpair, sbpair])
    near, snear = matrices(near), matrices(snear)
    both, bboth, far, bfar, bnear_b = gate([both, bboth, far, bfar, bnear_b], [near, snear, square])
    far = matrices(far)
    pnear, bpnear = around(both, "y"), around(bboth, "x")
    pfar, bpfar = across(far, link), across(bfar, zz)
    acc = product(plan[0], a_tiles, [share, near, snear, both])
    bnear_b, far = gate([bnear_b, far], [acc])
    sbnear_b, sbfar, sfar = swapped(bnear_b), swapped(bfar), swapped(far)
    pnear, bpnear, pfar, bpfar = gate([pnear, bpnear, pfar, bpfar], [acc, sfar, sbnear_b, sbfar])
    spnear, spfar, sbpfar, sbpnear = swapped(pnear), swapped(pfar), swapped(bpfar), swapped(bpnear)
    acc = product(plan[1], a_tiles, [pnear, far, sfar], acc)
    tables = [
        slab, bother, bnear_a, bnear_b, sbnear_a, sbnear_b, bfar, sbfar, bboth, bpnear, sbpnear, bpfar, sbpfar,
    ]
    pure, grid = final(plan[2], who, tile, row, col, a_tiles, [spnear, pfar, spfar], acc, square, tables)
    parts = lax.all_to_all(grid.reshape(128, 16), ROWS + BLK, split_axis=0, concat_axis=0, tiled=True)
    return pure.reshape(1, 1, C_TILES, BS * BS), jnp.sum(parts, axis=0)


def solution(mesh):
    split = Mesh(mesh.devices.reshape(4, 2, 2, 2, 4), ("x", "zh", "core", "zl", "y"))
    return jax.shard_map(
        body,
        mesh=split,
        in_specs=(
            P(ROWS, BLK, None, None),
            P(BLK, None, None),
            P(ROWS, BLK, None, None),
            P(ROWS, BLK, None, None, None),
            P(ROWS, BLK, None, None, None),
            P(ROWS, None, None, None),
        ),
        out_specs=(P(ROWS, BLK, None, None), P(ROWS + BLK)),
        check_vma=False,
    )
```
